512 devices in a mesh: ctx: 64 (over z, x), tp: 8 (over y, core).
Axes of the slice: x: 4, y: 4, z: 16, core: 2. Of those that a mesh axis runs over, the one named last changes fastest.
Arguments:
- doc_lengths: int32 [32], replicated, may hold values from 1 to 512, 8192 in all
- ssm_x: bfloat16 [8192, 8192], P('ctx', 'tp'), may hold values from -6 to 6
- ssm_gate: bfloat16 [8192, 8192], P('ctx', 'tp'), may hold values from -6 to 6
- ssm_b: bfloat16 [8192, 2048], P('ctx', 'tp'), may hold values from -6 to 6
- ssm_c: bfloat16 [8192, 2048], P('ctx', 'tp'), may hold values from -0.375 to 0.375
- step_size: float32 [8192, 128], P('ctx', 'tp'), as said below
- decay_rate: float32 [128], P('tp'), as said below
- norm_weight: float32 [8192], P('tp'), may hold values from 0.1 to 1.9
- queries: bfloat16 [8192, 8192], P('ctx', 'tp'), may hold values from -96 to 96
- keys: bfloat16 [8192, 1024], P('ctx', 'tp'), may hold values from -4 to 4
- values: bfloat16 [8192, 1024], P('ctx', 'tp'), may hold values from -6 to 6
Outputs:
- mixed: bfloat16 [8192, 8192], P(('ctx', 'tp'))
- attended: bfloat16 [8192, 8192], P(('ctx', 'tp'))
The draws below stay inside these ranges and needn't reach their ends.
Inputs may be any that keep to these rules, and one draw needn't show every extreme that they name: `doc_lengths`: every document has at least one token; the longest has exactly 512. `step_size`: Positive. `decay_rate`: Positive, at most 0.04.
All inputs are finite; a program needn't handle non-finite values.
Results may differ from the reference program's by a relative error of at most 0.0049.
Values may be sent and summed in bfloat16 or wider, within the bound.
No kernel may reach another device: no remote copies, remote signals or barrier semaphores. Data moves between devices by JAX's collectives and lax.ppermute only.
A program may use at most 192 MiB of HBM per device.

```python
import math
import jax
import jax.numpy as jnp
import numpy as np
from jax import lax

HEADS = 128
HEAD_DIM = 64
STATE = 256
GROUPS = 8
QHEADS = 64
KVHEADS = 8
ATT_DIM = 128
TOK_DEV = 128
NDOC = 32
SEQ = 8192
MAXDOC = 512


def log_uniform(key, out_shape, low_end, high_end):
    unit_draw = jax.random.uniform(key, out_shape, jnp.float32)
    return jnp.exp(math.log(low_end) + unit_draw * math.log(high_end / low_end))


def draw_decay_rate(key, part):
    head_order = jax.random.permutation(jax.random.fold_in(key, 11), HEADS)
    slow_rate = log_uniform(jax.random.fold_in(key, 12), (HEADS,), 0.3, 1.0) / MAXDOC
    fast_rate = log_uniform(jax.random.fold_in(key, 13), (HEADS,), 0.02, 0.04)
    fast_count = HEADS // 2
    return jnp.where(head_order < fast_count, fast_rate, slow_rate).astype(jnp.float32)


def draw_step_size(key, part):
    block_count = SEQ // TOK_DEV
    coarse = log_uniform(jax.random.fold_in(key, 21), (block_count, HEADS), 0.5, 2.0)
    fine_part = log_uniform(jax.random.fold_in(key, 22), (SEQ, HEADS), 0.5, 2.0)
    return (jnp.repeat(coarse, TOK_DEV, axis=0) * fine_part).astype(jnp.float32)


def attention_pair(key):
    base_key = jax.random.fold_in(key, 31)
    q_groups = QHEADS // KVHEADS
    keys_f = jnp.clip(jax.random.normal(jax.random.fold_in(base_key, 1), (SEQ, KVHEADS, ATT_DIM), jnp.float32), -4.0, 4.0)
    queries_f = jnp.clip(jax.random.normal(jax.random.fold_in(base_key, 2), (SEQ, KVHEADS, q_groups, ATT_DIM), jnp.float32), -4.0, 4.0)
    return (queries_f.reshape(SEQ, QHEADS * ATT_DIM), keys_f.reshape(SEQ, KVHEADS * ATT_DIM))


def draw_queries(key, part):
    return attention_pair(key)[0].astype(jnp.bfloat16)


def draw_keys(key, part):
    return attention_pair(key)[1].astype(jnp.bfloat16)


def shard_levels(own_key, extent, cuts, smallest, largest):
    def one(position, blocks):
        steps = jax.random.uniform(jax.random.fold_in(jax.random.fold_in(own_key, 6), position), (blocks,), jnp.float32, smallest / len(cuts), largest / len(cuts))
        return jnp.repeat(jnp.exp(steps), extent[position] // blocks).reshape((-1,) + (1,) * (len(extent) - position - 1))

    factor_of = one(*cuts[0])
    for cut in cuts[1:]:
        factor_of = factor_of * one(*cut)
    return factor_of


def profile(number_of, total, reach, lean):
    loads = [(1 << 20) // math.isqrt(rank ** lean) + 1 for rank in range(2, number_of + 1)]
    spare, holding = total - reach - (number_of - 1), [1] * (number_of - 1)
    while spare > 0:
        candidates = [i for i in range(number_of - 1) if holding[i] < reach]
        whole, remaining = sum([loads[i] for i in candidates]), spare
        for i in candidates:
            addition = min(reach - holding[i], max(1, remaining * loads[i] // whole), spare)
            holding[i] = holding[i] + addition
            spare = spare - addition
    return np.array([reach] + holding)


def ragged(stream_key, count, total, bound, lean):
    if count == 2:
        one = jax.random.randint(stream_key, (), max(1, total - bound), min(bound, total - 1) + 1)
        return jnp.stack([one, total - one])
    sizes = jnp.asarray(profile(count, total, bound, lean), jnp.int32)
    pairs = (count - 1) // 2
    donor, taker = sizes[1:1 + 2 * pairs:2], sizes[2:2 + 2 * pairs:2]
    slack = jnp.minimum(donor - 1, bound - taker)
    passed = jax.random.randint(jax.random.fold_in(stream_key, 1), (pairs,), 0, 1 << 20) % (slack + 1)
    sizes = sizes.at[1:1 + 2 * pairs:2].set(donor - passed).at[2:2 + 2 * pairs:2].set(taker + passed)
    return sizes[jax.random.permutation(jax.random.fold_in(stream_key, 2), count)]


def normal_values(stream_key, extent, scale, most, pieces=(), held_as=jnp.bfloat16):
    drawn = scale * jax.random.normal(stream_key, extent, jnp.float32)
    if pieces:
        drawn = drawn * shard_levels(stream_key, extent, pieces, -0.22, 0.18)
    return jnp.clip(drawn, -most, most).astype(held_as)


def setup_inputs(seed: int = 0) -> dict:
    streams_of = jax.random.split(jax.random.key(seed), 12)
    return {
        "doc_lengths": ragged(streams_of[0], NDOC, SEQ, MAXDOC, 2).astype(jnp.int32),
        "ssm_x": normal_values(streams_of[1], (SEQ, HEADS * HEAD_DIM), 1.0, 6.0, ((0, 64), (1, 8))),
        "ssm_gate": normal_values(streams_of[2], (SEQ, HEADS * HEAD_DIM), 1.0, 6.0, ((0, 64), (1, 8))),
        "ssm_b": normal_values(streams_of[3], (SEQ, GROUPS * STATE), 1.0, 6.0, ((0, 64), (1, 8))),
        "ssm_c": normal_values(streams_of[4], (SEQ, GROUPS * STATE), STATE ** -0.5, 0.375, ((0, 64), (1, 8))),
        "step_size": draw_step_size(jax.random.fold_in(streams_of[11], 71), 0),
        "decay_rate": draw_decay_rate(jax.random.fold_in(streams_of[11], 71), 0),
        "norm_weight": jnp.clip(1.0 + 0.18 * jax.random.normal(streams_of[7], (HEADS * HEAD_DIM,), jnp.float32), 0.1, 1.9),
        "queries": draw_queries(jax.random.fold_in(streams_of[11], 71), 0),
        "keys": draw_keys(jax.random.fold_in(streams_of[11], 71), 0),
        "values": normal_values(streams_of[10], (SEQ, KVHEADS * ATT_DIM), 1.0, 6.0, ((0, 64), (1, 8))),
    }


def doc_starts(doc_lengths):
    return (jnp.cumsum(doc_lengths) - doc_lengths).astype(jnp.int32)

def doc_index(positions, starts):
    return (lax.optimization_barrier(jnp.sum((starts[None, :] <= positions[:, None]).astype(jnp.int32), axis=1)) - 1).astype(jnp.int32)

def block_terms(ssm_x, ssm_b, ssm_c, step_size, decay_rate, doc_ids, prev_id, group_heads):
    tok_rows = ssm_x.shape[0]
    head_count = step_size.shape[1]
    group_count = head_count // group_heads
    head_size = ssm_x.shape[1] // head_count
    state_size = ssm_b.shape[1] // group_count
    inputs = ssm_x.reshape(tok_rows, group_count, group_heads, head_size)
    in_proj = ssm_b.reshape(tok_rows, group_count, state_size)
    out_proj = ssm_c.reshape(tok_rows, group_count, state_size)
    log_decay = -(step_size * decay_rate[None, :])
    cumulative = jnp.cumsum(log_decay, axis=0)
    same_doc = doc_ids[:, None] == doc_ids[None, :]
    causal = jnp.arange(tok_rows)[:, None] >= jnp.arange(tok_rows)[None, :]
    allowed = (same_doc & causal)[None]
    spread = cumulative.T[:, :, None] - cumulative.T[:, None, :]
    weights = jnp.where(allowed, jnp.exp(jnp.where(allowed, spread, 0.0)), 0.0) * step_size.T[:, None, :]
    intersection = jnp.einsum('tgn,sgn->gts', out_proj.astype(jnp.float32), in_proj.astype(jnp.float32))
    mixing = (weights.reshape(group_count, group_heads, tok_rows, tok_rows) * intersection[:, None]).astype(jnp.bfloat16)
    y_intra = jnp.einsum('ghts,sghp->tghp', mixing.astype(jnp.float32), inputs.astype(jnp.float32))
    final_sum = cumulative[-1]
    tail = jnp.exp(final_sum[None, :] - cumulative) * step_size * (doc_ids == doc_ids[-1]).astype(jnp.float32)[:, None]
    scaled = (inputs.astype(jnp.float32) * tail.reshape(tok_rows, group_count, group_heads)[..., None]).astype(jnp.bfloat16)
    state_local = jnp.einsum('sghp,sgn->ghpn', scaled.astype(jnp.float32), in_proj.astype(jnp.float32))
    entry = jnp.exp(cumulative) * (doc_ids == prev_id).astype(jnp.float32)[:, None]
    transmit = jnp.exp(final_sum) * (doc_ids[-1] == prev_id).astype(jnp.float32)
    return (y_intra, state_local, entry, transmit.reshape(group_count, group_heads))

def finish_rows(y_intra, entry, carried, ssm_c, ssm_gate, norm_weight):
    tok_rows, group_count, group_heads, head_size = y_intra.shape
    out_proj = ssm_c.reshape(tok_rows, group_count, -1).astype(jnp.float32)
    incoming = jnp.einsum('tgn,ghpn->tghp', out_proj, carried, precision=lax.Precision.HIGHEST)
    mixer_out = y_intra + incoming * entry.reshape(tok_rows, group_count, group_heads)[..., None]
    gate_vals = ssm_gate.reshape(tok_rows, group_count, group_heads, head_size).astype(jnp.float32)
    gated = (mixer_out * jax.nn.silu(gate_vals)).reshape(tok_rows, group_count, group_heads * head_size)
    factor = lax.rsqrt(lax.optimization_barrier(jnp.mean(gated * gated, axis=2, keepdims=True)) + 1e-05)
    return ((gated * factor).reshape(tok_rows, -1) * norm_weight[None, :]).astype(jnp.bfloat16)

def take_rows(array, begin, count):
    return lax.dynamic_slice_in_dim(array, begin, count, 0)

def reference(doc_lengths, ssm_x, ssm_gate, ssm_b, ssm_c, step_size, decay_rate, norm_weight, queries, keys, values):
    starts = doc_starts(doc_lengths)
    block_count = SEQ // TOK_DEV
    group_heads = HEADS // GROUPS

    def mixer_block(carried, block_index):
        begin = (block_index * TOK_DEV).astype(jnp.int32)
        positions = begin + jnp.arange(TOK_DEV, dtype=jnp.int32)
        doc_ids = doc_index(positions, starts)
        prev_id = doc_index(jnp.reshape(begin - 1, (1,)).astype(jnp.int32), starts)[0]
        y_intra, state_local, entry, transmit = block_terms(take_rows(ssm_x, begin, TOK_DEV), take_rows(ssm_b, begin, TOK_DEV), take_rows(ssm_c, begin, TOK_DEV), take_rows(step_size, begin, TOK_DEV), decay_rate, doc_ids, prev_id, group_heads)
        rows_out = finish_rows(y_intra, entry, carried, take_rows(ssm_c, begin, TOK_DEV), take_rows(ssm_gate, begin, TOK_DEV), norm_weight)
        return (transmit[:, :, None, None] * carried + state_local, rows_out)
    start_state = jnp.zeros((GROUPS, group_heads, HEAD_DIM, STATE), jnp.float32)
    unused_state, mixed_blocks = lax.scan(mixer_block, start_state, jnp.arange(block_count, dtype=jnp.int32))
    mixed = mixed_blocks.reshape(SEQ, HEADS * HEAD_DIM)
    q_groups = QHEADS // KVHEADS
    window = MAXDOC + TOK_DEV
    scale = ATT_DIM ** (-0.5)

    def attention_block(block_index):
        begin = (block_index * TOK_DEV).astype(jnp.int32)
        window_begin = jnp.maximum(begin - MAXDOC, 0).astype(jnp.int32)
        query_rows = take_rows(queries, begin, TOK_DEV).reshape(TOK_DEV, KVHEADS, q_groups, ATT_DIM).astype(jnp.float32)
        key_rows = take_rows(keys, window_begin, window).reshape(window, KVHEADS, ATT_DIM).astype(jnp.float32)
        value_rows = take_rows(values, window_begin, window).reshape(window, KVHEADS, ATT_DIM).astype(jnp.float32)
        query_pos = begin + jnp.arange(TOK_DEV, dtype=jnp.int32)
        key_pos = window_begin + jnp.arange(window, dtype=jnp.int32)
        allowed = (doc_index(query_pos, starts)[:, None] == doc_index(key_pos, starts)[None, :]) & (key_pos[None, :] <= query_pos[:, None])
        scores = jnp.einsum('tngd,knd->ngtk', query_rows, key_rows) * scale
        scores = jnp.where(allowed[None, None], scores, -jnp.inf)
        top_score = lax.optimization_barrier(jnp.max(scores, axis=3, keepdims=True))
        probs = jnp.exp(scores - top_score)
        total = lax.optimization_barrier(jnp.sum(probs, axis=3))
        rounded = lax.optimization_barrier(probs.astype(jnp.bfloat16))
        summed = jnp.einsum('ngtk,knd->ngtd', rounded.astype(jnp.float32), value_rows)
        result = summed / total[..., None]
        return jnp.transpose(result, (2, 0, 1, 3)).reshape(TOK_DEV, -1).astype(jnp.bfloat16)
    attended = lax.map(attention_block, jnp.arange(block_count, dtype=jnp.int32)).reshape(SEQ, QHEADS * ATT_DIM)
    return (mixed, attended)
```

```python
import functools

import jax
import jax.numpy as jnp
from jax import lax
from jax.experimental import pallas as pl
from jax.experimental.pallas import tpu as pltpu
from jax.sharding import Mesh, PartitionSpec as P

ROWS = 128
HALF = 64
GROUP_HEADS = 16
Q_HEADS = 8
PEERS = 4
STATE = 256
SCALE = 128**-0.5
NEG = -1e30
F32 = jnp.float32
BF16 = jnp.bfloat16
VMEM = pl.BlockSpec(memory_space=pltpu.VMEM)
SMEM = pl.BlockSpec(memory_space=pltpu.SMEM)


def call(kernel, outs, specs, flops=0, moved=0, exps=0):
    return pl.pallas_call(
        kernel,
        out_shape=outs,
        in_specs=specs,
        out_specs=jax.tree.map(lambda _: VMEM, outs),
        compiler_params=pltpu.CompilerParams(vmem_limit_bytes=32 * 2**20),
        cost_estimate=pl.CostEstimate(flops=flops, bytes_accessed=moved, transcendentals=exps),
    )


def shaped(shape, dtype):
    return jax.ShapeDtypeStruct(shape, dtype)


def dot(a, b, dims=((1,), (0,)), precision=None):
    return lax.dot_general(
        a, b, (dims, ((), ())), precision=precision, preferred_element_type=F32
    )


def three_parts(a):
    high = a.astype(BF16)
    rest = a - high.astype(F32)
    middle = rest.astype(BF16)
    low = (rest - middle.astype(F32)).astype(BF16)
    return high, middle, low


def start_row(doc_ref, begin):
    pos = begin + lax.broadcasted_iota(jnp.int32, (8, ROWS), 1)
    found = jnp.zeros((8, ROWS), jnp.int32)
    last = jnp.int32(0)
    start = jnp.int32(0)
    for j in range(doc_ref.shape[0]):
        found = jnp.where(pos >= start, start, found)
        last = jnp.where(begin + ROWS - 1 >= start, start, last)
        start = start + doc_ref[j]
    return found, last


def head_rows(dt_ref, rate_ref):
    row = lax.broadcasted_iota(jnp.int32, (GROUP_HEADS, ROWS), 0)
    rate = jnp.zeros((GROUP_HEADS, ROWS), F32)
    for h in range(GROUP_HEADS):
        rate = jnp.where(row == h, rate_ref[h], rate)
    dt = dt_ref[...]
    upto = lax.broadcasted_iota(jnp.int32, (ROWS, ROWS), 0) <= lax.broadcasted_iota(
        jnp.int32, (ROWS, ROWS), 1
    )
    decay = -(dt * rate)
    upto = upto.astype(F32).astype(BF16)
    total = sum(dot(part, upto) for part in three_parts(decay))
    return dt, total


def spread_heads(parts):
    width = GROUP_HEADS * HALF
    lane = lax.broadcasted_iota(jnp.int32, (GROUP_HEADS, width), 1)
    row = lax.broadcasted_iota(jnp.int32, (GROUP_HEADS, width), 0)
    pick = ((lane >= row * HALF) & (lane < (row + 1) * HALF)).astype(F32).astype(BF16)
    return sum(dot(part, pick, ((0,), (0,))) for part in parts)


def prepare(doc_ref, begin_ref, rate_ref, x_ref, b_ref, dt_ref, k_ref, v_ref, out_ref, kv_ref):
    begin = begin_ref[0]
    _, last_start = start_row(doc_ref, begin)
    dt, total = head_rows(dt_ref, rate_ref)
    final = total[:, ROWS - 1 :]
    pos = begin + lax.broadcasted_iota(jnp.int32, (GROUP_HEADS, ROWS), 1)
    tail = jnp.where(pos >= last_start, jnp.exp(final - total) * dt, 0.0)
    tail = spread_heads(three_parts(tail))
    scaled = (x_ref[...].astype(F32) * tail).astype(BF16)
    whole = jnp.broadcast_to(final, (GROUP_HEADS, ROWS))
    transmit = jnp.where(last_start < begin, jnp.exp(whole), 0.0)
    parts = three_parts(spread_heads([p[:, :16] for p in three_parts(transmit)]))
    row = lax.broadcasted_iota(jnp.int32, (16, GROUP_HEADS * HALF), 0)
    sent = jnp.where(
        row == 0,
        parts[0].astype(F32),
        jnp.where(row == 1, parts[1].astype(F32), parts[2].astype(F32)),
    ).astype(BF16)
    state = dot(b_ref[...], scaled, ((0,), (0,))).astype(BF16)
    width = GROUP_HEADS * HALF // PEERS
    for j in range(PEERS):
        out_ref[j, :STATE, :] = state[:, j * width : (j + 1) * width]
        out_ref[j, STATE:, :] = sent[:, j * width : (j + 1) * width]
    kv_ref[:, :ROWS] = k_ref[...]
    kv_ref[:, ROWS:] = v_ref[...]


def received(ref, j):
    state = ref[j, :STATE, :].astype(F32)
    parts = ref[j, STATE:, :].astype(F32)
    return state, parts[0:1] + parts[1:2] + parts[2:3]


def group_state(got_ref, kv_ref, out_ref):
    total, _ = received(got_ref, 0)
    for j in range(1, PEERS):
        state, transmit = received(got_ref, j)
        total = total * transmit + state
    out_ref[:STATE, :] = total.astype(BF16)
    out_ref[STATE:, :] = kv_ref[...]


def carried_states(got_ref, before_ref, out_ref):
    carried = before_ref[:STATE, :].astype(F32)
    for j in range(PEERS):
        out_ref[j] = carried.astype(BF16)
        if j < PEERS - 1:
            state, transmit = received(got_ref, j)
            carried = carried * transmit + state


def start_columns(doc_ref, begin):
    found, _ = start_row(doc_ref, begin)
    return jnp.transpose(jnp.broadcast_to(found[:1].astype(F32), (ROWS, ROWS)))


def inside(doc_ref, begin_ref, rate_ref, x_ref, b_ref, c_ref, dt_ref, gate_ref, own_ref, factor_ref):
    begin = begin_ref[0]
    starts = start_columns(doc_ref, begin)
    row = lax.broadcasted_iota(jnp.int32, (ROWS, ROWS), 0)
    lane = lax.broadcasted_iota(jnp.int32, (ROWS, ROWS), 1)
    allowed = (lane <= row) & ((begin + lane).astype(F32) >= starts)
    continued = starts < begin.astype(F32)
    dt, total = head_rows(dt_ref, rate_ref)
    tall = jnp.transpose(jnp.concatenate([total, jnp.zeros((ROWS - GROUP_HEADS, ROWS), F32)], 0))
    inner = dot(c_ref[...], b_ref[...], ((1,), (1,)))
    left = lane < HALF
    for pair in range(GROUP_HEADS // 2):
        at = slice(pair * ROWS, (pair + 1) * ROWS)
        columns, mixing = [], []
        for h in (2 * pair, 2 * pair + 1):
            column = jnp.broadcast_to(tall[:, h : h + 1], (ROWS, ROWS))
            spread = jnp.where(allowed, column - total[h : h + 1], NEG)
            mixing.append((jnp.exp(spread) * dt[h : h + 1] * inner).astype(BF16))
            columns.append(column)
        x = x_ref[:, at]
        zero = jnp.zeros_like(x)
        blocks = jnp.concatenate([jnp.where(left, x, zero), jnp.where(left, zero, x)], 0)
        own = dot(jnp.concatenate(mixing, 1), blocks)
        entry = jnp.where(continued, jnp.exp(jnp.where(left, columns[0], columns[1])), 0.0)
        gate = gate_ref[:, at].astype(F32)
        gate = gate / (1.0 + jnp.exp(-gate))
        own_ref[:, at] = own * gate
        factor_ref[:, at] = entry * gate


def attention(doc_ref, begin_ref, q_ref, kv0_ref, kv1_ref, kv2_ref, kv3_ref, kv4_ref, out_ref):
    begin = begin_ref[0]
    starts = start_columns(doc_ref, begin)
    row = lax.broadcasted_iota(jnp.int32, (ROWS, ROWS), 0)
    lane = lax.broadcasted_iota(jnp.int32, (ROWS, ROWS), 1)
    blocks = [kv0_ref[...], kv1_ref[...], kv2_ref[...], kv3_ref[...], kv4_ref[STATE:, :]]
    bias = []
    for j in range(len(blocks)):
        allowed = (begin - j * ROWS + lane).astype(F32) >= starts
        if j == 0:
            allowed = allowed & (lane <= row)
        bias.append(jnp.where(allowed, 0.0, NEG))
    bias = jnp.concatenate(bias, 1)
    keys = jnp.concatenate([b[:, :ROWS] for b in blocks], 0)
    values = jnp.concatenate([b[:, ROWS:] for b in blocks], 0)
    for h in range(Q_HEADS):
        at = slice(h * ROWS, (h + 1) * ROWS)
        scores = dot(q_ref[:, at], keys, ((1,), (1,))) * SCALE + bias
        top = jnp.max(scores, axis=1, keepdims=True)
        probs = jnp.exp(scores - top)
        total = jnp.sum(probs, axis=1, keepdims=True)
        out_ref[:, at] = (dot(probs.astype(BF16), values) / total).astype(BF16)


def finish(c_ref, carried_ref, own_ref, factor_ref, weight_ref, att_ref, out_ref, scratch_ref):
    width = GROUP_HEADS * HALF // PEERS
    squares = jnp.zeros((ROWS, 1), F32)
    c = c_ref[...]
    for j in range(PEERS):
        at = slice(j * width, (j + 1) * width)
        gated = own_ref[:, at] + factor_ref[:, at] * dot(c, carried_ref[j])
        scratch_ref[:, at] = gated
        squares = squares + jnp.sum(gated * gated, axis=1, keepdims=True)
    scale = lax.rsqrt(squares * (1.0 / (GROUP_HEADS * HALF)) + 1e-05)
    for j in range(PEERS):
        at = slice(j * width, (j + 1) * width)
        out_ref[:, at] = (scratch_ref[:, at] * scale * weight_ref[:, at]).astype(BF16)
    out_ref[:, GROUP_HEADS * HALF :] = att_ref[...]


def lay_out(got_ref, mixed_ref, attended_ref):
    width = GROUP_HEADS * HALF
    for j in range(got_ref.shape[0]):
        mixed_ref[:, j * width : (j + 1) * width] = got_ref[j, :, :width]
        attended_ref[:, j * width : (j + 1) * width] = got_ref[j, :, width:]


def local(doc, x, gate, b, c, dt, rate, weight, q, k, v):
    width = GROUP_HEADS * HALF
    tp = lax.axis_size("tp")
    block = lax.axis_index("z") * PEERS + lax.axis_index("x")
    begin = jnp.reshape(block * ROWS, (1,)).astype(jnp.int32)
    dt = dt.T
    own_states, kv = call(
        prepare,
        (shaped((PEERS, STATE + 16, width // PEERS), BF16), shaped((ROWS, 2 * ROWS), BF16)),
        [SMEM, SMEM, SMEM] + [VMEM] * 5,
        flops=10**8,
        moved=10**6,
    )(doc, begin, rate, x, b, dt, k, v)
    got = lax.all_to_all(own_states, "x", 0, 0, tiled=True)

    def along(a, distance):
        count = lax.axis_size("z") * PEERS
        return lax.ppermute(a, ("z", "x"), [(i - distance, i) for i in range(distance, count)])

    near = [along(kv, d) for d in range(1, PEERS)]
    group = call(
        group_state,
        shaped((STATE + ROWS, width // PEERS), BF16),
        [VMEM] * 2,
        flops=10**6,
        moved=10**6,
    )(got, kv)
    before = lax.ppermute(group, "z", [(i - 1, i) for i in range(1, lax.axis_size("z"))])
    carried = call(
        carried_states,
        shaped((PEERS, STATE, width // PEERS), BF16),
        [VMEM] * 2,
        flops=10**6,
        moved=10**6,
    )(got, before)
    carried = lax.all_to_all(carried, "x", 0, 0, tiled=True)
    own, factor = call(
        inside,
        (shaped((ROWS, width), F32), shaped((ROWS, width), F32)),
        [SMEM, SMEM, SMEM] + [VMEM] * 5,
        flops=10**8,
        moved=10**6,
        exps=400000,
    )(doc, begin, rate, x, b, c, dt, gate)
    att = call(
        attention,
        shaped((ROWS, width), BF16),
        [SMEM, SMEM] + [VMEM] * 6,
        flops=4 * 10**8,
        moved=10**6,
        exps=700000,
    )(doc, begin, q, kv, *near, before)
    rows = pl.pallas_call(
        finish,
        out_shape=shaped((ROWS, 2 * width), BF16),
        in_specs=[VMEM] * 6,
        out_specs=VMEM,
        scratch_shapes=[pltpu.VMEM((ROWS, width), F32)],
        compiler_params=pltpu.CompilerParams(vmem_limit_bytes=32 * 2**20),
        cost_estimate=pl.CostEstimate(flops=10**8, bytes_accessed=10**6, transcendentals=128),
    )(c, carried, own, factor, weight.reshape(1, width), att)
    moved = lax.all_to_all(rows.reshape(tp, ROWS // tp, 2 * width), "tp", 0, 0, tiled=True)
    return call(
        lay_out,
        (shaped((ROWS // tp, tp * width), BF16), shaped((ROWS // tp, tp * width), BF16)),
        [VMEM],
        moved=10**6,
    )(moved)


def solution(mesh):
    sizes = dict(mesh.shape)
    inner = Mesh(
        mesh.devices.reshape(sizes["ctx"] // PEERS, PEERS, sizes["tp"]), ("z", "x", "tp")
    )
    both = P(("z", "x"), "tp")
    return jax.shard_map(
        local,
        mesh=inner,
        in_specs=(P(), both, both, both, both, both, P("tp"), P("tp"), both, both, both),
        out_specs=(P(("z", "x", "tp"), None), P(("z", "x", "tp"), None)),
        check_vma=False,
    )
```

```python
import functools

import jax
import jax.numpy as jnp
from jax import lax
from jax.experimental import pallas as pl
from jax.experimental.pallas import tpu as pltpu
from jax.sharding import Mesh, PartitionSpec as P

ROWS = 128
HALF = 64
GROUP_HEADS = 16
Q_HEADS = 8
PEERS = 4
STATE = 256
SCALE = 128**-0.5
NEG = -1e30
F32 = jnp.float32
BF16 = jnp.bfloat16
VMEM = pl.BlockSpec(memory_space=pltpu.VMEM)
SMEM = pl.BlockSpec(memory_space=pltpu.SMEM)
HBM = pl.BlockSpec(memory_space=pltpu.HBM)
LATER = pl.BlockSpec(memory_space=pl.ANY)


def call(kernel, outs, specs, flops=0, moved=0, exps=0, scratch=(), grant=32 * 2**20):
    return pl.pallas_call(
        kernel,
        out_shape=outs,
        in_specs=specs,
        scratch_shapes=scratch,
        out_specs=jax.tree.map(lambda _: VMEM, outs),
        compiler_params=pltpu.CompilerParams(vmem_limit_bytes=grant),
        cost_estimate=pl.CostEstimate(flops=flops, bytes_accessed=moved, transcendentals=exps),
    )


def shaped(shape, dtype):
    return jax.ShapeDtypeStruct(shape, dtype)


def dot(a, b, dims=((1,), (0,)), precision=None):
    return lax.dot_general(
        a, b, (dims, ((), ())), precision=precision, preferred_element_type=F32
    )


def three_parts(a):
    high = a.astype(BF16)
    rest = a - high.astype(F32)
    middle = rest.astype(BF16)
    low = (rest - middle.astype(F32)).astype(BF16)
    return high, middle, low


def start_row(doc_ref, begin):
    pos = begin + lax.broadcasted_iota(jnp.int32, (8, ROWS), 1)
    found = jnp.zeros((8, ROWS), jnp.int32)
    last = jnp.int32(0)
    start = jnp.int32(0)
    for j in range(doc_ref.shape[0]):
        found = jnp.where(pos >= start, start, found)
        last = jnp.where(begin + ROWS - 1 >= start, start, last)
        start = start + doc_ref[j]
    return found, last


def head_rows(dt_ref, rate_ref):
    row = lax.broadcasted_iota(jnp.int32, (GROUP_HEADS, ROWS), 0)
    rate = jnp.zeros((GROUP_HEADS, ROWS), F32)
    for h in range(GROUP_HEADS):
        rate = jnp.where(row == h, rate_ref[h], rate)
    dt = dt_ref[...]
    upto = lax.broadcasted_iota(jnp.int32, (ROWS, ROWS), 0) <= lax.broadcasted_iota(
        jnp.int32, (ROWS, ROWS), 1
    )
    decay = -(dt * rate)
    upto = upto.astype(F32).astype(BF16)
    total = sum(dot(part, upto) for part in three_parts(decay))
    return dt, total


def spread_heads(parts):
    width = GROUP_HEADS * HALF
    lane = lax.broadcasted_iota(jnp.int32, (GROUP_HEADS, width), 1)
    row = lax.broadcasted_iota(jnp.int32, (GROUP_HEADS, width), 0)
    pick = ((lane >= row * HALF) & (lane < (row + 1) * HALF)).astype(F32).astype(BF16)
    return sum(dot(part, pick, ((0,), (0,))) for part in parts)


def prepare(
    begin_ref,
    doc_hbm,
    rate_hbm,
    dt_hbm,
    x_hbm,
    b_hbm,
    k_hbm,
    v_hbm,
    out_ref,
    kv_ref,
    doc_ref,
    rate_ref,
    dt_ref,
    x_ref,
    b_ref,
    sems,
):
    pairs = (
        (doc_hbm, doc_ref),
        (rate_hbm, rate_ref),
        (dt_hbm, dt_ref),
        (x_hbm, x_ref),
        (b_hbm, b_ref),
        (k_hbm, kv_ref.at[:, :ROWS]),
        (v_hbm, kv_ref.at[:, ROWS:]),
    )
    copies = [pltpu.make_async_copy(s, d, sems.at[i]) for i, (s, d) in enumerate(pairs)]
    for copy in copies:
        copy.start()
    begin = begin_ref[0]
    for copy in copies[:3]:
        copy.wait()
    _, last_start = start_row(doc_ref, begin)
    dt, total = head_rows(dt_ref, rate_ref)
    final = total[:, ROWS - 1 :]
    pos = begin + lax.broadcasted_iota(jnp.int32, (GROUP_HEADS, ROWS), 1)
    tail = jnp.where(pos >= last_start, jnp.exp(final - total) * dt, 0.0)
    tail = spread_heads(three_parts(tail))
    copies[3].wait()
    scaled = (x_ref[...].astype(F32) * tail).astype(BF16)
    whole = jnp.broadcast_to(final, (GROUP_HEADS, ROWS))
    transmit = jnp.where(last_start < begin, jnp.exp(whole), 0.0)
    parts = three_parts(spread_heads([p[:, :16] for p in three_parts(transmit)]))
    row = lax.broadcasted_iota(jnp.int32, (16, GROUP_HEADS * HALF), 0)
    sent = jnp.where(
        row == 0,
        parts[0].astype(F32),
        jnp.where(row == 1, parts[1].astype(F32), parts[2].astype(F32)),
    ).astype(BF16)
    copies[4].wait()
    state = dot(b_ref[...], scaled, ((0,), (0,))).astype(BF16)
    width = GROUP_HEADS * HALF // PEERS
    for j in range(PEERS):
        out_ref[j, :STATE, :] = state[:, j * width : (j + 1) * width]
        out_ref[j, STATE:, :] = sent[:, j * width : (j + 1) * width]
    for copy in copies[5:]:
        copy.wait()


def received(ref, j):
    state = ref[j, :STATE, :].astype(F32)
    parts = ref[j, STATE:, :].astype(F32)
    return state, parts[0:1] + parts[1:2] + parts[2:3]


def pair_up(kv_ref, near_ref, pair_ref):
    pair_ref[:ROWS, :] = kv_ref[...]
    pair_ref[ROWS:, :] = near_ref[...]


def group_state(got_ref, kv_ref, near_ref, out_ref):
    del near_ref
    total, _ = received(got_ref, 0)
    for j in range(1, PEERS):
        state, transmit = received(got_ref, j)
        total = total * transmit + state
    out_ref[:STATE, :] = total.astype(BF16)
    out_ref[STATE:, :] = kv_ref[...]


def carried_states(got_ref, before_ref, out_ref):
    carried = before_ref[:STATE, :].astype(F32)
    for j in range(PEERS):
        out_ref[j] = carried.astype(BF16)
        if j < PEERS - 1:
            state, transmit = received(got_ref, j)
            carried = carried * transmit + state


def start_columns(doc_ref, begin):
    found, _ = start_row(doc_ref, begin)
    return jnp.transpose(jnp.broadcast_to(found[:1].astype(F32), (ROWS, ROWS)))


def inside(
    begin_ref,
    doc_ref,
    rate_ref,
    x_ref,
    b_ref,
    c_ref,
    dt_ref,
    gate_ref,
    gain_ref,
    carried_ref,
    own_ref,
    factor_ref,
    gain_out_ref,
):
    del carried_ref
    begin = begin_ref[0]
    gain_out_ref[...] = gain_ref[...]
    starts = start_columns(doc_ref, begin)
    row = lax.broadcasted_iota(jnp.int32, (ROWS, ROWS), 0)
    lane = lax.broadcasted_iota(jnp.int32, (ROWS, ROWS), 1)
    allowed = (lane <= row) & ((begin + lane).astype(F32) >= starts)
    continued = starts < begin.astype(F32)
    dt, total = head_rows(dt_ref, rate_ref)
    tall = jnp.transpose(jnp.concatenate([total, jnp.zeros((ROWS - GROUP_HEADS, ROWS), F32)], 0))
    inner = dot(c_ref[...], b_ref[...], ((1,), (1,)))
    left = lane < HALF
    for pair in range(GROUP_HEADS // 2):
        at = slice(pair * ROWS, (pair + 1) * ROWS)
        columns, mixing = [], []
        for h in (2 * pair, 2 * pair + 1):
            column = jnp.broadcast_to(tall[:, h : h + 1], (ROWS, ROWS))
            spread = jnp.where(allowed, column - total[h : h + 1], NEG)
            mixing.append((jnp.exp(spread) * dt[h : h + 1] * inner).astype(BF16))
            columns.append(column)
        x = x_ref[:, at]
        zero = jnp.zeros_like(x)
        blocks = jnp.concatenate([jnp.where(left, x, zero), jnp.where(left, zero, x)], 0)
        own = dot(jnp.concatenate(mixing, 1), blocks)
        entry = jnp.where(continued, jnp.exp(jnp.where(left, columns[0], columns[1])), 0.0)
        gate = gate_ref[:, at].astype(F32)
        gate = gate / (1.0 + jnp.exp(-gate))
        own_ref[:, at] = own * gate
        factor_ref[:, at] = entry * gate


def attention(begin_ref, doc_ref, q_ref, kv0_ref, kv1_ref, pair_ref, kv4_ref, out_ref):
    begin = begin_ref[0]
    starts = start_columns(doc_ref, begin)
    row = lax.broadcasted_iota(jnp.int32, (ROWS, ROWS), 0)
    lane = lax.broadcasted_iota(jnp.int32, (ROWS, ROWS), 1)
    blocks = [kv0_ref[...], kv1_ref[...], pair_ref[:ROWS, :], pair_ref[ROWS:, :], kv4_ref[STATE:, :]]
    bias = []
    for j in range(len(blocks)):
        allowed = (begin - j * ROWS + lane).astype(F32) >= starts
        if j == 0:
            allowed = allowed & (lane <= row)
        bias.append(jnp.where(allowed, 0.0, NEG))
    bias = jnp.concatenate(bias, 1)
    keys = jnp.concatenate([b[:, :ROWS] for b in blocks], 0)
    values = jnp.concatenate([b[:, ROWS:] for b in blocks], 0)
    for h in range(Q_HEADS):
        at = slice(h * ROWS, (h + 1) * ROWS)
        scores = dot(q_ref[:, at], keys, ((1,), (1,))) * SCALE + bias
        top = jnp.max(scores, axis=1, keepdims=True)
        probs = jnp.exp(scores - top)
        total = jnp.sum(probs, axis=1, keepdims=True)
        out_ref[:, at] = (dot(probs.astype(BF16), values) / total).astype(BF16)


def finish(c_ref, carried_ref, own_ref, factor_ref, weight_ref, att_ref, out_ref, scratch_ref):
    width = GROUP_HEADS * HALF // PEERS
    squares = jnp.zeros((ROWS, 1), F32)
    c = c_ref[...]
    for j in range(PEERS):
        at = slice(j * width, (j + 1) * width)
        gated = own_ref[:, at] + factor_ref[:, at] * dot(c, carried_ref[j])
        scratch_ref[:, at] = gated
        squares = squares + jnp.sum(gated * gated, axis=1, keepdims=True)
    scale = lax.rsqrt(squares * (1.0 / (GROUP_HEADS * HALF)) + 1e-05)
    for j in range(PEERS):
        at = slice(j * width, (j + 1) * width)
        out_ref[:, at] = (scratch_ref[:, at] * scale * weight_ref[:, at]).astype(BF16)
    out_ref[:, GROUP_HEADS * HALF :] = att_ref[...]


def lay_out(got_ref, mixed_ref, attended_ref):
    width = GROUP_HEADS * HALF
    for j in range(got_ref.shape[0]):
        mixed_ref[:, j * width : (j + 1) * width] = got_ref[j, :, :width]
        attended_ref[:, j * width : (j + 1) * width] = got_ref[j, :, width:]


def local(doc, x, gate, b, c, dt, rate, weight, q, k, v):
    width = GROUP_HEADS * HALF
    tp = lax.axis_size("tp")
    block = lax.axis_index("z") * PEERS + lax.axis_index("x")
    begin = jnp.reshape(block * ROWS, (1,)).astype(jnp.int32)
    dt = dt.T
    own_states, kv = call(
        prepare,
        (shaped((PEERS, STATE + 16, width // PEERS), BF16), shaped((ROWS, 2 * ROWS), BF16)),
        [SMEM] + [HBM] * 7,
        flops=10**8,
        moved=10**6,
        scratch=(
            pltpu.SMEM(doc.shape, jnp.int32),
            pltpu.SMEM(rate.shape, F32),
            pltpu.VMEM(dt.shape, F32),
            pltpu.VMEM(x.shape, BF16),
            pltpu.VMEM(b.shape, BF16),
            pltpu.SemaphoreType.DMA((7,)),
        ),
        grant=None,
    )(begin, doc, rate, dt, x, b, k, v)
    got = lax.all_to_all(own_states, "x", 0, 0, tiled=True)

    def along(a, distance):
        count = lax.axis_size("z") * PEERS
        return lax.ppermute(a, ("z", "x"), [(i - distance, i) for i in range(distance, count)])

    kv1 = along(kv, 1)
    pair = call(pair_up, shaped((2 * ROWS, 2 * ROWS), BF16), [VMEM] * 2, moved=10**8)(kv, kv1)
    pair = along(pair, 2)
    group = call(
        group_state,
        shaped((STATE + ROWS, width // PEERS), BF16),
        [VMEM] * 2 + [LATER],
        flops=10**6,
        moved=10**6,
    )(got, kv, kv1)
    before = lax.ppermute(group, "z", [(i - 1, i) for i in range(1, lax.axis_size("z"))])
    carried = call(
        carried_states,
        shaped((PEERS, STATE, width // PEERS), BF16),
        [VMEM] * 2,
        flops=10**6,
        moved=10**6,
    )(got, before)
    own, factor, gain = call(
        inside,
        (shaped((ROWS, width), F32), shaped((ROWS, width), F32), shaped((1, width), F32)),
        [SMEM, SMEM, SMEM] + [VMEM] * 6 + [LATER],
        flops=10**8,
        moved=10**6,
        exps=400000,
    )(begin, doc, rate, x, b, c, dt, gate, weight.reshape(1, width), carried)
    carried = lax.all_to_all(carried, "x", 0, 0, tiled=True)
    att = call(
        attention,
        shaped((ROWS, width), BF16),
        [SMEM, SMEM] + [VMEM] * 5,
        flops=10**10,
        moved=10**8,
        exps=10**8,
    )(begin, doc, q, kv, kv1, pair, before)
    rows = pl.pallas_call(
        finish,
        out_shape=shaped((ROWS, 2 * width), BF16),
        in_specs=[VMEM] * 6,
        out_specs=VMEM,
        scratch_shapes=[pltpu.VMEM((ROWS, width), F32)],
        compiler_params=pltpu.CompilerParams(vmem_limit_bytes=32 * 2**20),
        cost_estimate=pl.CostEstimate(flops=10**8, bytes_accessed=10**6, transcendentals=128),
    )(c, carried, own, factor, gain, att)
    moved = lax.all_to_all(rows.reshape(tp, ROWS // tp, 2 * width), "tp", 0, 0, tiled=True)
    return call(
        lay_out,
        (shaped((ROWS // tp, tp * width), BF16), shaped((ROWS // tp, tp * width), BF16)),
        [VMEM],
        moved=10**6,
    )(moved)


def solution(mesh):
    sizes = dict(mesh.shape)
    inner = Mesh(
        mesh.devices.reshape(sizes["ctx"] // PEERS, PEERS, sizes["tp"]), ("z", "x", "tp")
    )
    both = P(("z", "x"), "tp")
    return jax.shard_map(
        local,
        mesh=inner,
        in_specs=(P(), both, both, both, both, both, P("tp"), P("tp"), both, both, both),
        out_specs=(P(("z", "x", "tp"), None), P(("z", "x", "tp"), None)),
        check_vma=False,
    )
```

```python
import functools

import jax
import jax.numpy as jnp
from jax import lax
from jax.experimental import pallas as pl
from jax.experimental.pallas import tpu as pltpu
from jax.sharding import Mesh, PartitionSpec as P

ROWS = 128
HALF = 64
GROUP_HEADS = 16
Q_HEADS = 8
PEERS = 4
STATE = 256
SCALE = 128**-0.5
NEG = -1e30
F32 = jnp.float32
BF16 = jnp.bfloat16
VMEM = pl.BlockSpec(memory_space=pltpu.VMEM)
SMEM = pl.BlockSpec(memory_space=pltpu.SMEM)
HBM = pl.BlockSpec(memory_space=pltpu.HBM)
LATER = pl.BlockSpec(memory_space=pl.ANY)


def call(kernel, outs, specs, flops=0, moved=0, exps=0, scratch=(), grant=32 * 2**20, out=VMEM):
    return pl.pallas_call(
        kernel,
        out_shape=outs,
        in_specs=specs,
        scratch_shapes=scratch,
        out_specs=jax.tree.map(lambda _: out, outs),
        compiler_params=pltpu.CompilerParams(vmem_limit_bytes=grant),
        cost_estimate=pl.CostEstimate(flops=flops, bytes_accessed=moved, transcendentals=exps),
    )


def shaped(shape, dtype):
    return jax.ShapeDtypeStruct(shape, dtype)


def dot(a, b, dims=((1,), (0,)), precision=None):
    return lax.dot_general(
        a, b, (dims, ((), ())), precision=precision, preferred_element_type=F32
    )


def three_parts(a):
    high = a.astype(BF16)
    rest = a - high.astype(F32)
    middle = rest.astype(BF16)
    low = (rest - middle.astype(F32)).astype(BF16)
    return high, middle, low


def start_row(doc_ref, begin):
    pos = begin + lax.broadcasted_iota(jnp.int32, (8, ROWS), 1)
    found = jnp.zeros((8, ROWS), jnp.int32)
    last = jnp.int32(0)
    start = jnp.int32(0)
    for j in range(doc_ref.shape[0]):
        found = jnp.where(pos >= start, start, found)
        last = jnp.where(begin + ROWS - 1 >= start, start, last)
        start = start + doc_ref[j]
    return found, last


def head_rows(dt_ref, rate_ref):
    row = lax.broadcasted_iota(jnp.int32, (GROUP_HEADS, ROWS), 0)
    rate = jnp.zeros((GROUP_HEADS, ROWS), F32)
    for h in range(GROUP_HEADS):
        rate = jnp.where(row == h, rate_ref[h], rate)
    dt = dt_ref[...]
    upto = lax.broadcasted_iota(jnp.int32, (ROWS, ROWS), 0) <= lax.broadcasted_iota(
        jnp.int32, (ROWS, ROWS), 1
    )
    upto = upto.astype(F32).astype(BF16)
    sums = dot(jnp.concatenate(three_parts(-(dt * rate)), 0), upto)
    total = sums[:GROUP_HEADS] + sums[GROUP_HEADS : 2 * GROUP_HEADS] + sums[2 * GROUP_HEADS :]
    return dt, total


def spread_heads(a):
    width = GROUP_HEADS * HALF
    lane = lax.broadcasted_iota(jnp.int32, (3 * GROUP_HEADS, width), 1)
    row = lax.broadcasted_iota(jnp.int32, (3 * GROUP_HEADS, width), 0) & (GROUP_HEADS - 1)
    pick = ((lane >= row * HALF) & (lane < (row + 1) * HALF)).astype(F32).astype(BF16)
    return dot(jnp.concatenate(three_parts(a), 0), pick, ((0,), (0,)))


def prepare(
    begin_ref,
    doc_hbm,
    rate_hbm,
    dt_hbm,
    x_hbm,
    b_hbm,
    k_hbm,
    v_hbm,
    out_hbm,
    kv_hbm,
    doc_ref,
    rate_ref,
    dt_ref,
    x_ref,
    b_ref,
    kv_ref,
    out_ref,
    sems,
):
    pairs = (
        (doc_hbm, doc_ref),
        (rate_hbm, rate_ref),
        (dt_hbm, dt_ref),
        (b_hbm, b_ref),
        (x_hbm, x_ref),
        (k_hbm, kv_ref.at[:, :ROWS]),
        (v_hbm, kv_ref.at[:, ROWS:]),
        (kv_ref, kv_hbm),
        (out_ref.at[0], out_hbm.at[0]),
        (out_ref.at[1], out_hbm.at[1]),
        (out_ref.at[2], out_hbm.at[2]),
        (out_ref.at[3], out_hbm.at[3]),
    )
    copies = [pltpu.make_async_copy(s, d, sems.at[i]) for i, (s, d) in enumerate(pairs)]
    for copy in copies[:7]:
        copy.start()
    begin = begin_ref[0]
    for copy in copies[:3]:
        copy.wait()
    _, last_start = start_row(doc_ref, begin)
    dt, total = head_rows(dt_ref, rate_ref)
    final = total[:, ROWS - 1 :]
    pos = begin + lax.broadcasted_iota(jnp.int32, (GROUP_HEADS, ROWS), 1)
    tail = jnp.where(pos >= last_start, jnp.exp(final - total) * dt, 0.0)
    tail = spread_heads(tail)
    whole = jnp.broadcast_to(final, (GROUP_HEADS, ROWS))
    transmit = jnp.where(last_start < begin, jnp.exp(whole), 0.0)
    parts = three_parts(spread_heads(transmit)[:16])
    row = lax.broadcasted_iota(jnp.int32, (16, GROUP_HEADS * HALF), 0)
    sent = jnp.where(
        row == 0,
        parts[0].astype(F32),
        jnp.where(row == 1, parts[1].astype(F32), parts[2].astype(F32)),
    ).astype(BF16)
    copies[3].wait()
    turned = jnp.transpose(b_ref[...])
    copies[4].wait()
    width = GROUP_HEADS * HALF // PEERS
    for j in range(PEERS):
        at = slice(j * width, (j + 1) * width)
        scaled = (x_ref[:, at].astype(F32) * tail[:, at]).astype(BF16)
        out_ref[j, :STATE, :] = dot(turned, scaled).astype(BF16)
        out_ref[j, STATE:, :] = sent[:, at]
        copies[8 + j].start()
    for copy in copies[5:7]:
        copy.wait()
    copies[7].start()
    for copy in copies[7:]:
        copy.wait()


def received(ref, j):
    state = ref[j, :STATE, :].astype(F32)
    parts = ref[j, STATE:, :].astype(F32)
    return state, parts[0:1] + parts[1:2] + parts[2:3]


def pair_up(kv_ref, near_ref, pair_ref):
    pair_ref[:ROWS, :] = kv_ref[...]
    pair_ref[ROWS:, :] = near_ref[...]


def group_state(got_ref, kv_ref, near_ref, out_ref):
    del near_ref
    total, _ = received(got_ref, 0)
    for j in range(1, PEERS):
        state, transmit = received(got_ref, j)
        total = total * transmit + state
    out_ref[:STATE, :] = total.astype(BF16)
    out_ref[STATE:, :] = kv_ref[...]


def carried_states(got_ref, before_ref, out_hbm, out_ref, sems):
    carried = before_ref[:STATE, :].astype(F32)
    copies = []
    for j in range(PEERS):
        out_ref[j] = carried.astype(BF16)
        copies.append(pltpu.make_async_copy(out_ref.at[j], out_hbm.at[j], sems.at[j]))
        copies[j].start()
        if j < PEERS - 1:
            state, transmit = received(got_ref, j)
            carried = carried * transmit + state
    for copy in copies:
        copy.wait()


def start_columns(doc_ref, begin):
    found, _ = start_row(doc_ref, begin)
    return jnp.transpose(jnp.broadcast_to(found[:1].astype(F32), (ROWS, ROWS)))


def inside(
    begin_ref,
    doc_ref,
    rate_ref,
    x_ref,
    b_ref,
    c_ref,
    dt_ref,
    gate_ref,
    gain_ref,
    carried_ref,
    own_ref,
    factor_ref,
    gain_out_ref,
):
    del carried_ref
    begin = begin_ref[0]
    gain_out_ref[...] = gain_ref[...]
    starts = start_columns(doc_ref, begin)
    row = lax.broadcasted_iota(jnp.int32, (ROWS, ROWS), 0)
    lane = lax.broadcasted_iota(jnp.int32, (ROWS, ROWS), 1)
    allowed = (lane <= row) & ((begin + lane).astype(F32) >= starts)
    continued = starts < begin.astype(F32)
    dt, total = head_rows(dt_ref, rate_ref)
    tall = jnp.transpose(jnp.concatenate([total, jnp.zeros((ROWS - GROUP_HEADS, ROWS), F32)], 0))
    inner = dot(c_ref[...], b_ref[...], ((1,), (1,)))
    left = lane < HALF
    for pair in range(GROUP_HEADS // 2):
        at = slice(pair * ROWS, (pair + 1) * ROWS)
        columns, mixing = [], []
        for h in (2 * pair, 2 * pair + 1):
            column = jnp.broadcast_to(tall[:, h : h + 1], (ROWS, ROWS))
            spread = jnp.where(allowed, column - total[h : h + 1], NEG)
            mixing.append((jnp.exp(spread) * dt[h : h + 1] * inner).astype(BF16))
            columns.append(column)
        x = x_ref[:, at]
        zero = jnp.zeros_like(x)
        blocks = jnp.concatenate([jnp.where(left, x, zero), jnp.where(left, zero, x)], 0)
        own = dot(jnp.concatenate(mixing, 1), blocks)
        entry = jnp.where(continued, jnp.exp(jnp.where(left, columns[0], columns[1])), 0.0)
        gate = gate_ref[:, at].astype(F32)
        gate = gate / (1.0 + jnp.exp(-gate))
        own_ref[:, at] = own * gate
        factor_ref[:, at] = entry * gate


def attention(begin_ref, doc_ref, q_ref, kv0_ref, kv1_ref, pair_ref, kv4_ref, out_ref):
    begin = begin_ref[0]
    starts = start_columns(doc_ref, begin)
    row = lax.broadcasted_iota(jnp.int32, (ROWS, ROWS), 0)
    lane = lax.broadcasted_iota(jnp.int32, (ROWS, ROWS), 1)
    blocks = [kv0_ref[...], kv1_ref[...], pair_ref[:ROWS, :], pair_ref[ROWS:, :], kv4_ref[STATE:, :]]
    bias = []
    for j in range(len(blocks)):
        allowed = (begin - j * ROWS + lane).astype(F32) >= starts
        if j == 0:
            allowed = allowed & (lane <= row)
        bias.append(jnp.where(allowed, 0.0, NEG))
    bias = jnp.concatenate(bias, 1)
    keys = jnp.concatenate([b[:, :ROWS] for b in blocks], 0)
    values = jnp.concatenate([b[:, ROWS:] for b in blocks], 0)
    for h in range(Q_HEADS):
        at = slice(h * ROWS, (h + 1) * ROWS)
        scores = dot(q_ref[:, at], keys, ((1,), (1,))) * SCALE + bias
        top = jnp.max(scores, axis=1, keepdims=True)
        probs = jnp.exp(scores - top)
        total = jnp.sum(probs, axis=1, keepdims=True)
        out_ref[:, at] = (dot(probs.astype(BF16), values) / total).astype(BF16)


def finish(c_ref, carried_ref, own_ref, factor_ref, weight_ref, att_ref, out_ref, scratch_ref):
    width = GROUP_HEADS * HALF // PEERS
    squares = jnp.zeros((ROWS, 1), F32)
    c = c_ref[...]
    for j in range(PEERS):
        at = slice(j * width, (j + 1) * width)
        gated = own_ref[:, at] + factor_ref[:, at] * dot(c, carried_ref[j])
        scratch_ref[:, at] = gated
        squares = squares + jnp.sum(gated * gated, axis=1, keepdims=True)
    scale = lax.rsqrt(squares * (1.0 / (GROUP_HEADS * HALF)) + 1e-05)
    for j in range(PEERS):
        at = slice(j * width, (j + 1) * width)
        out_ref[:, at] = (scratch_ref[:, at] * scale * weight_ref[:, at]).astype(BF16)
    out_ref[:, GROUP_HEADS * HALF :] = att_ref[...]


def lay_out(got_ref, mixed_ref, attended_ref):
    width = GROUP_HEADS * HALF
    for j in range(got_ref.shape[0]):
        mixed_ref[:, j * width : (j + 1) * width] = got_ref[j, :, :width]
        attended_ref[:, j * width : (j + 1) * width] = got_ref[j, :, width:]


def local(doc, x, gate, b, c, dt, rate, weight, q, k, v):
    width = GROUP_HEADS * HALF
    tp = lax.axis_size("tp")
    block = lax.axis_index("z") * PEERS + lax.axis_index("x")
    begin = jnp.reshape(block * ROWS, (1,)).astype(jnp.int32)
    dt = dt.T
    own_states, kv = call(
        prepare,
        (shaped((PEERS, STATE + 16, width // PEERS), BF16), shaped((ROWS, 2 * ROWS), BF16)),
        [SMEM] + [HBM] * 7,
        flops=10**8,
        moved=10**6,
        scratch=(
            pltpu.SMEM(doc.shape, jnp.int32),
            pltpu.SMEM(rate.shape, F32),
            pltpu.VMEM(dt.shape, F32),
            pltpu.VMEM(x.shape, BF16),
            pltpu.VMEM(b.shape, BF16),
            pltpu.VMEM((ROWS, 2 * ROWS), BF16),
            pltpu.VMEM((PEERS, STATE + 16, width // PEERS), BF16),
            pltpu.SemaphoreType.DMA((12,)),
        ),
        grant=None,
        out=HBM,
    )(begin, doc, rate, dt, x, b, k, v)
    got = lax.all_to_all(own_states, "x", 0, 0, tiled=True)

    def along(a, distance):
        count = lax.axis_size("z") * PEERS
        return lax.ppermute(a, ("z", "x"), [(i - distance, i) for i in range(distance, count)])

    kv1 = along(kv, 1)
    pair = call(pair_up, shaped((2 * ROWS, 2 * ROWS), BF16), [VMEM] * 2, moved=10**8)(kv, kv1)
    pair = along(pair, 2)
    group = call(
        group_state,
        shaped((STATE + ROWS, width // PEERS), BF16),
        [VMEM] * 2 + [LATER],
        flops=10**6,
        moved=10**6,
    )(got, kv, kv1)
    before = lax.ppermute(group, "z", [(i - 1, i) for i in range(1, lax.axis_size("z"))])
    carried = call(
        carried_states,
        shaped((PEERS, STATE, width // PEERS), BF16),
        [VMEM] * 2,
        flops=10**6,
        moved=10**6,
        scratch=(
            pltpu.VMEM((PEERS, STATE, width // PEERS), BF16),
            pltpu.SemaphoreType.DMA((PEERS,)),
        ),
        out=HBM,
    )(got, before)
    own, factor, gain = call(
        inside,
        (shaped((ROWS, width), F32), shaped((ROWS, width), F32), shaped((1, width), F32)),
        [SMEM, SMEM, SMEM] + [VMEM] * 6 + [LATER],
        flops=10**8,
        moved=10**6,
        exps=400000,
    )(begin, doc, rate, x, b, c, dt, gate, weight.reshape(1, width), carried)
    carried = lax.all_to_all(carried, "x", 0, 0, tiled=True)
    att = call(
        attention,
        shaped((ROWS, width), BF16),
        [SMEM, SMEM] + [VMEM] * 5,
        flops=10**10,
        moved=10**8,
        exps=10**8,
    )(begin, doc, q, kv, kv1, pair, before)
    rows = pl.pallas_call(
        finish,
        out_shape=shaped((ROWS, 2 * width), BF16),
        in_specs=[VMEM] * 6,
        out_specs=VMEM,
        scratch_shapes=[pltpu.VMEM((ROWS, width), F32)],
        compiler_params=pltpu.CompilerParams(vmem_limit_bytes=32 * 2**20),
        cost_estimate=pl.CostEstimate(flops=10**8, bytes_accessed=10**6, transcendentals=128),
    )(c, carried, own, factor, gain, att)
    moved = lax.all_to_all(rows.reshape(tp, ROWS // tp, 2 * width), "tp", 0, 0, tiled=True)
    return call(
        lay_out,
        (shaped((ROWS // tp, tp * width), BF16), shaped((ROWS // tp, tp * width), BF16)),
        [VMEM],
        moved=10**6,
    )(moved)


def solution(mesh):
    sizes = dict(mesh.shape)
    inner = Mesh(
        mesh.devices.reshape(sizes["ctx"] // PEERS, PEERS, sizes["tp"]), ("z", "x", "tp")
    )
    both = P(("z", "x"), "tp")
    return jax.shard_map(
        local,
        mesh=inner,
        in_specs=(P(), both, both, both, both, both, P("tp"), P("tp"), both, both, both),
        out_specs=(P(("z", "x", "tp"), None), P(("z", "x", "tp"), None)),
        check_vma=False,
    )
```

```python
import functools

import jax
import jax.numpy as jnp
from jax import lax
from jax.experimental import pallas as pl
from jax.experimental.pallas import tpu as pltpu
from jax.sharding import Mesh, PartitionSpec as P

ROWS = 128
HALF = 64
GROUP_HEADS = 16
Q_HEADS = 8
PEERS = 4
STATE = 256
SCALE = 128**-0.5
NEG = -1e30
F32 = jnp.float32
BF16 = jnp.bfloat16
VMEM = pl.BlockSpec(memory_space=pltpu.VMEM)
SMEM = pl.BlockSpec(memory_space=pltpu.SMEM)
HBM = pl.BlockSpec(memory_space=pltpu.HBM)
LATER = pl.BlockSpec(memory_space=pl.ANY)


def call(kernel, outs, specs, flops=0, moved=0, exps=0, scratch=(), grant=32 * 2**20, out=VMEM):
    return pl.pallas_call(
        kernel,
        out_shape=outs,
        in_specs=specs,
        scratch_shapes=scratch,
        out_specs=jax.tree.map(lambda _: out, outs),
        compiler_params=pltpu.CompilerParams(vmem_limit_bytes=grant),
        cost_estimate=pl.CostEstimate(flops=flops, bytes_accessed=moved, transcendentals=exps),
    )


def shaped(shape, dtype):
    return jax.ShapeDtypeStruct(shape, dtype)


def dot(a, b, dims=((1,), (0,)), precision=None):
    return lax.dot_general(
        a, b, (dims, ((), ())), precision=precision, preferred_element_type=F32
    )


def three_parts(a):
    high = a.astype(BF16)
    rest = a - high.astype(F32)
    middle = rest.astype(BF16)
    low = (rest - middle.astype(F32)).astype(BF16)
    return high, middle, low


def start_row(doc_ref, begin):
    pos = begin + lax.broadcasted_iota(jnp.int32, (8, ROWS), 1)
    found = jnp.zeros((8, ROWS), jnp.int32)
    last = jnp.int32(0)
    start = jnp.int32(0)
    for j in range(doc_ref.shape[0]):
        found = jnp.where(pos >= start, start, found)
        last = jnp.where(begin + ROWS - 1 >= start, start, last)
        start = start + doc_ref[j]
    return found, last


def head_rows(dt_ref, rate_ref):
    row = lax.broadcasted_iota(jnp.int32, (GROUP_HEADS, ROWS), 0)
    rate = jnp.zeros((GROUP_HEADS, ROWS), F32)
    for h in range(GROUP_HEADS):
        rate = jnp.where(row == h, rate_ref[h], rate)
    dt = dt_ref[...]
    upto = lax.broadcasted_iota(jnp.int32, (ROWS, ROWS), 0) <= lax.broadcasted_iota(
        jnp.int32, (ROWS, ROWS), 1
    )
    upto = upto.astype(F32).astype(BF16)
    sums = dot(jnp.concatenate(three_parts(-(dt * rate)), 0), upto)
    total = sums[:GROUP_HEADS] + sums[GROUP_HEADS : 2 * GROUP_HEADS] + sums[2 * GROUP_HEADS :]
    return dt, total


def spread_heads(a):
    width = GROUP_HEADS * HALF
    lane = lax.broadcasted_iota(jnp.int32, (3 * GROUP_HEADS, width), 1)
    row = lax.broadcasted_iota(jnp.int32, (3 * GROUP_HEADS, width), 0) & (GROUP_HEADS - 1)
    pick = ((lane >= row * HALF) & (lane < (row + 1) * HALF)).astype(F32).astype(BF16)
    return dot(jnp.concatenate(three_parts(a), 0), pick, ((0,), (0,)))


def prepare(
    begin_ref,
    doc_hbm,
    rate_hbm,
    dt_hbm,
    x_hbm,
    b_hbm,
    k_hbm,
    v_hbm,
    out_hbm,
    kv_hbm,
    doc_ref,
    rate_ref,
    dt_ref,
    x_ref,
    b_ref,
    kv_ref,
    out_ref,
    sems,
):
    pairs = (
        (doc_hbm, doc_ref),
        (rate_hbm, rate_ref),
        (dt_hbm, dt_ref),
        (b_hbm, b_ref),
        (x_hbm, x_ref),
        (k_hbm, kv_ref.at[:, :ROWS]),
        (v_hbm, kv_ref.at[:, ROWS:]),
        (kv_ref, kv_hbm),
        (out_ref.at[0], out_hbm.at[0]),
        (out_ref.at[1], out_hbm.at[1]),
        (out_ref.at[2], out_hbm.at[2]),
        (out_ref.at[3], out_hbm.at[3]),
    )
    copies = [pltpu.make_async_copy(s, d, sems.at[i]) for i, (s, d) in enumerate(pairs)]
    for copy in copies[:7]:
        copy.start()
    begin = begin_ref[0]
    for copy in copies[:3]:
        copy.wait()
    _, last_start = start_row(doc_ref, begin)
    dt, total = head_rows(dt_ref, rate_ref)
    final = total[:, ROWS - 1 :]
    pos = begin + lax.broadcasted_iota(jnp.int32, (GROUP_HEADS, ROWS), 1)
    tail = jnp.where(pos >= last_start, jnp.exp(final - total) * dt, 0.0)
    tail = spread_heads(tail)
    whole = jnp.broadcast_to(final, (GROUP_HEADS, ROWS))
    transmit = jnp.where(last_start < begin, jnp.exp(whole), 0.0)
    parts = three_parts(spread_heads(transmit)[:16])
    row = lax.broadcasted_iota(jnp.int32, (16, GROUP_HEADS * HALF), 0)
    sent = jnp.where(
        row == 0,
        parts[0].astype(F32),
        jnp.where(row == 1, parts[1].astype(F32), parts[2].astype(F32)),
    ).astype(BF16)
    copies[3].wait()
    turned = jnp.transpose(b_ref[...])
    copies[4].wait()
    width = GROUP_HEADS * HALF // PEERS
    for j in range(PEERS):
        at = slice(j * width, (j + 1) * width)
        scaled = (x_ref[:, at].astype(F32) * tail[:, at]).astype(BF16)
        out_ref[j, :STATE, :] = dot(turned, scaled).astype(BF16)
        out_ref[j, STATE:, :] = sent[:, at]
        copies[8 + j].start()
    for copy in copies[5:7]:
        copy.wait()
    copies[7].start()
    for copy in copies[7:]:
        copy.wait()


def received(ref, j):
    state = ref[j, :STATE, :].astype(F32)
    parts = ref[j, STATE:, :].astype(F32)
    return state, parts[0:1] + parts[1:2] + parts[2:3]


def pair_up(kv_ref, near_ref, pair_ref):
    pair_ref[:ROWS, :] = kv_ref[...]
    pair_ref[ROWS:, :] = near_ref[...]


def group_state(got_ref, kv_ref, near_ref, own_ref, out_ref):
    del near_ref, own_ref
    total, _ = received(got_ref, 0)
    for j in range(1, PEERS):
        state, transmit = received(got_ref, j)
        total = total * transmit + state
    out_ref[:STATE, :] = total.astype(BF16)
    out_ref[STATE:, :] = kv_ref[...]


def carried_states(got_ref, before_ref, out_hbm, out_ref, sems):
    copies = [
        pltpu.make_async_copy(out_ref.at[j], out_hbm.at[j], sems.at[j]) for j in range(PEERS)
    ]
    out_ref[0] = before_ref[:STATE, :]
    copies[0].start()
    carried = before_ref[:STATE, :].astype(F32)
    for j in range(1, PEERS):
        state, transmit = received(got_ref, j - 1)
        carried = carried * transmit + state
        out_ref[j] = carried.astype(BF16)
        copies[j].start()
    for copy in copies:
        copy.wait()


def start_columns(doc_ref, begin):
    found, _ = start_row(doc_ref, begin)
    return jnp.transpose(jnp.broadcast_to(found[:1].astype(F32), (ROWS, ROWS)))


def inside(
    begin_ref,
    doc_ref,
    rate_ref,
    x_ref,
    b_ref,
    c_ref,
    dt_ref,
    gate_ref,
    gain_ref,
    own_ref,
    factor_ref,
    gain_out_ref,
):
    begin = begin_ref[0]
    gain_out_ref[...] = gain_ref[...]
    starts = start_columns(doc_ref, begin)
    row = lax.broadcasted_iota(jnp.int32, (ROWS, ROWS), 0)
    lane = lax.broadcasted_iota(jnp.int32, (ROWS, ROWS), 1)
    allowed = (lane <= row) & ((begin + lane).astype(F32) >= starts)
    continued = starts < begin.astype(F32)
    dt, total = head_rows(dt_ref, rate_ref)
    tall = jnp.transpose(jnp.concatenate([total, jnp.zeros((ROWS - GROUP_HEADS, ROWS), F32)], 0))
    inner = dot(c_ref[...], b_ref[...], ((1,), (1,)))
    left = lane < HALF
    for pair in range(GROUP_HEADS // 2):
        at = slice(pair * ROWS, (pair + 1) * ROWS)
        columns, mixing = [], []
        for h in (2 * pair, 2 * pair + 1):
            column = jnp.broadcast_to(tall[:, h : h + 1], (ROWS, ROWS))
            spread = jnp.where(allowed, column - total[h : h + 1], NEG)
            mixing.append((jnp.exp(spread) * dt[h : h + 1] * inner).astype(BF16))
            columns.append(column)
        x = x_ref[:, at]
        zero = jnp.zeros_like(x)
        blocks = jnp.concatenate([jnp.where(left, x, zero), jnp.where(left, zero, x)], 0)
        own = dot(jnp.concatenate(mixing, 1), blocks)
        entry = jnp.where(continued, jnp.exp(jnp.where(left, columns[0], columns[1])), 0.0)
        gate = gate_ref[:, at].astype(F32)
        gate = gate / (1.0 + jnp.exp(-gate))
        own_ref[:, at] = own * gate
        factor_ref[:, at] = entry * gate


def attention(begin_ref, doc_ref, q_ref, kv0_ref, kv2_ref, pair_ref, kv4_ref, out_ref):
    begin = begin_ref[0]
    starts = start_columns(doc_ref, begin)
    row = lax.broadcasted_iota(jnp.int32, (ROWS, ROWS), 0)
    lane = lax.broadcasted_iota(jnp.int32, (ROWS, ROWS), 1)
    blocks = [kv0_ref[...], pair_ref[:ROWS, :], kv2_ref[...], pair_ref[ROWS:, :], kv4_ref[STATE:, :]]
    bias = []
    for j in range(len(blocks)):
        allowed = (begin - j * ROWS + lane).astype(F32) >= starts
        if j == 0:
            allowed = allowed & (lane <= row)
        bias.append(jnp.where(allowed, 0.0, NEG))
    bias = jnp.concatenate(bias, 1)
    keys = jnp.concatenate([b[:, :ROWS] for b in blocks], 0)
    values = jnp.concatenate([b[:, ROWS:] for b in blocks], 0)
    for h in range(Q_HEADS):
        at = slice(h * ROWS, (h + 1) * ROWS)
        scores = dot(q_ref[:, at], keys, ((1,), (1,))) * SCALE + bias
        top = jnp.max(scores, axis=1, keepdims=True)
        probs = jnp.exp(scores - top)
        total = jnp.sum(probs, axis=1, keepdims=True)
        out_ref[:, at] = (dot(probs.astype(BF16), values) / total).astype(BF16)


def finish(c_ref, carried_ref, own_ref, factor_ref, weight_ref, att_ref, out_ref, scratch_ref):
    width = GROUP_HEADS * HALF // PEERS
    squares = jnp.zeros((ROWS, 1), F32)
    c = c_ref[...]
    for j in range(PEERS):
        at = slice(j * width, (j + 1) * width)
        gated = own_ref[:, at] + factor_ref[:, at] * dot(c, carried_ref[j])
        scratch_ref[:, at] = gated
        squares = squares + jnp.sum(gated * gated, axis=1, keepdims=True)
    scale = lax.rsqrt(squares * (1.0 / (GROUP_HEADS * HALF)) + 1e-05)
    for j in range(PEERS):
        at = slice(j * width, (j + 1) * width)
        out_ref[:, at] = (scratch_ref[:, at] * scale * weight_ref[:, at]).astype(BF16)
    out_ref[:, GROUP_HEADS * HALF :] = att_ref[...]


def lay_out(got_ref, mixed_ref, attended_ref):
    width = GROUP_HEADS * HALF
    for j in range(got_ref.shape[0]):
        mixed_ref[:, j * width : (j + 1) * width] = got_ref[j, :, :width]
        attended_ref[:, j * width : (j + 1) * width] = got_ref[j, :, width:]


def local(doc, x, gate, b, c, dt, rate, weight, q, k, v):
    width = GROUP_HEADS * HALF
    tp = lax.axis_size("tp")
    block = lax.axis_index("z") * PEERS + lax.axis_index("x")
    begin = jnp.reshape(block * ROWS, (1,)).astype(jnp.int32)
    dt = dt.T
    own_states, kv = call(
        prepare,
        (shaped((PEERS, STATE + 16, width // PEERS), BF16), shaped((ROWS, 2 * ROWS), BF16)),
        [SMEM] + [HBM] * 7,
        flops=10**8,
        moved=10**6,
        scratch=(
            pltpu.SMEM(doc.shape, jnp.int32),
            pltpu.SMEM(rate.shape, F32),
            pltpu.VMEM(dt.shape, F32),
            pltpu.VMEM(x.shape, BF16),
            pltpu.VMEM(b.shape, BF16),
            pltpu.VMEM((ROWS, 2 * ROWS), BF16),
            pltpu.VMEM((PEERS, STATE + 16, width // PEERS), BF16),
            pltpu.SemaphoreType.DMA((12,)),
        ),
        grant=None,
        out=HBM,
    )(begin, doc, rate, dt, x, b, k, v)
    got = lax.all_to_all(own_states, "x", 0, 0, tiled=True)

    def along(a, distance):
        count = lax.axis_size("z") * PEERS
        return lax.ppermute(a, ("z", "x"), [(i - distance, i) for i in range(distance, count)])

    kv2 = along(kv, 2)
    pair = call(pair_up, shaped((2 * ROWS, 2 * ROWS), BF16), [VMEM] * 2, moved=10**8)(kv, kv2)
    pair = along(pair, 1)
    own, factor, gain = call(
        inside,
        (shaped((ROWS, width), F32), shaped((ROWS, width), F32), shaped((1, width), F32)),
        [SMEM, SMEM, SMEM] + [VMEM] * 6,
        flops=10**8,
        moved=10**6,
        exps=400000,
    )(begin, doc, rate, x, b, c, dt, gate, weight.reshape(1, width))
    group = call(
        group_state,
        shaped((STATE + ROWS, width // PEERS), BF16),
        [VMEM] * 2 + [LATER] * 2,
        flops=10**6,
        moved=10**6,
    )(got, kv, kv2, own)
    before = lax.ppermute(group, "z", [(i - 1, i) for i in range(1, lax.axis_size("z"))])
    carried = call(
        carried_states,
        shaped((PEERS, STATE, width // PEERS), BF16),
        [VMEM] * 2,
        flops=10**6,
        moved=10**6,
        scratch=(
            pltpu.VMEM((PEERS, STATE, width // PEERS), BF16),
            pltpu.SemaphoreType.DMA((PEERS,)),
        ),
        out=HBM,
    )(got, before)
    carried = lax.all_to_all(carried, "x", 0, 0, tiled=True)
    att = call(
        attention,
        shaped((ROWS, width), BF16),
        [SMEM, SMEM] + [VMEM] * 5,
        flops=10**10,
        moved=10**8,
        exps=10**8,
    )(begin, doc, q, kv, kv2, pair, before)
    rows = pl.pallas_call(
        finish,
        out_shape=shaped((ROWS, 2 * width), BF16),
        in_specs=[VMEM] * 6,
        out_specs=VMEM,
        scratch_shapes=[pltpu.VMEM((ROWS, width), F32)],
        compiler_params=pltpu.CompilerParams(vmem_limit_bytes=32 * 2**20),
        cost_estimate=pl.CostEstimate(flops=10**8, bytes_accessed=10**6, transcendentals=128),
    )(c, carried, own, factor, gain, att)
    moved = lax.all_to_all(rows.reshape(tp, ROWS // tp, 2 * width), "tp", 0, 0, tiled=True)
    return call(
        lay_out,
        (shaped((ROWS // tp, tp * width), BF16), shaped((ROWS // tp, tp * width), BF16)),
        [VMEM],
        moved=10**6,
    )(moved)


def solution(mesh):
    sizes = dict(mesh.shape)
    inner = Mesh(
        mesh.devices.reshape(sizes["ctx"] // PEERS, PEERS, sizes["tp"]), ("z", "x", "tp")
    )
    both = P(("z", "x"), "tp")
    return jax.shard_map(
        local,
        mesh=inner,
        in_specs=(P(), both, both, both, both, both, P("tp"), P("tp"), both, both, both),
        out_specs=(P(("z", "x", "tp"), None), P(("z", "x", "tp"), None)),
        check_vma=False,
    )
```

```python
import functools

import jax
import jax.numpy as jnp
from jax import lax
from jax.experimental import pallas as pl
from jax.experimental.pallas import tpu as pltpu
from jax.sharding import Mesh, PartitionSpec as P

ROWS = 128
HALF = 64
GROUP_HEADS = 16
Q_HEADS = 8
PEERS = 4
STATE = 256
SCALE = 128**-0.5
NEG = -1e30
F32 = jnp.float32
BF16 = jnp.bfloat16
VMEM = pl.BlockSpec(memory_space=pltpu.VMEM)
SMEM = pl.BlockSpec(memory_space=pltpu.SMEM)
HBM = pl.BlockSpec(memory_space=pltpu.HBM)
LATER = pl.BlockSpec(memory_space=pl.ANY)


def call(kernel, outs, specs, flops=0, moved=0, exps=0, scratch=(), grant=32 * 2**20, out=VMEM):
    return pl.pallas_call(
        kernel,
        out_shape=outs,
        in_specs=specs,
        scratch_shapes=scratch,
        out_specs=jax.tree.map(lambda _: out, outs),
        compiler_params=pltpu.CompilerParams(vmem_limit_bytes=grant),
        cost_estimate=pl.CostEstimate(flops=flops, bytes_accessed=moved, transcendentals=exps),
    )


def shaped(shape, dtype):
    return jax.ShapeDtypeStruct(shape, dtype)


def dot(a, b, dims=((1,), (0,)), precision=None):
    return lax.dot_general(
        a, b, (dims, ((), ())), precision=precision, preferred_element_type=F32
    )


def three_parts(a):
    high = a.astype(BF16)
    rest = a - high.astype(F32)
    middle = rest.astype(BF16)
    low = (rest - middle.astype(F32)).astype(BF16)
    return high, middle, low


def start_row(doc_ref, begin):
    pos = begin + lax.broadcasted_iota(jnp.int32, (8, ROWS), 1)
    found = jnp.zeros((8, ROWS), jnp.int32)
    last = jnp.int32(0)
    start = jnp.int32(0)
    for j in range(doc_ref.shape[0]):
        found = jnp.where(pos >= start, start, found)
        last = jnp.where(begin + ROWS - 1 >= start, start, last)
        start = start + doc_ref[j]
    return found, last


def head_rows(dt_ref, rate_ref):
    row = lax.broadcasted_iota(jnp.int32, (GROUP_HEADS, ROWS), 0)
    rate = jnp.zeros((GROUP_HEADS, ROWS), F32)
    for h in range(GROUP_HEADS):
        rate = jnp.where(row == h, rate_ref[h], rate)
    dt = dt_ref[...]
    upto = lax.broadcasted_iota(jnp.int32, (ROWS, ROWS), 0) <= lax.broadcasted_iota(
        jnp.int32, (ROWS, ROWS), 1
    )
    upto = upto.astype(F32).astype(BF16)
    sums = dot(jnp.concatenate(three_parts(-(dt * rate)), 0), upto)
    total = sums[:GROUP_HEADS] + sums[GROUP_HEADS : 2 * GROUP_HEADS] + sums[2 * GROUP_HEADS :]
    return dt, total


def spread_heads(a):
    width = GROUP_HEADS * HALF
    lane = lax.broadcasted_iota(jnp.int32, (3 * GROUP_HEADS, width), 1)
    row = lax.broadcasted_iota(jnp.int32, (3 * GROUP_HEADS, width), 0) & (GROUP_HEADS - 1)
    pick = ((lane >= row * HALF) & (lane < (row + 1) * HALF)).astype(F32).astype(BF16)
    return dot(jnp.concatenate(three_parts(a), 0), pick, ((0,), (0,)))


def prepare(
    begin_ref,
    doc_hbm,
    rate_hbm,
    dt_hbm,
    x_hbm,
    b_hbm,
    k_hbm,
    v_hbm,
    out_hbm,
    kv_hbm,
    doc_ref,
    rate_ref,
    dt_ref,
    x_ref,
    b_ref,
    kv_ref,
    out_ref,
    sems,
):
    pairs = (
        (doc_hbm, doc_ref),
        (rate_hbm, rate_ref),
        (dt_hbm, dt_ref),
        (b_hbm, b_ref),
        (x_hbm, x_ref),
        (k_hbm, kv_ref.at[:, :ROWS]),
        (v_hbm, kv_ref.at[:, ROWS:]),
        (kv_ref, kv_hbm),
        (out_ref.at[0], out_hbm.at[0]),
        (out_ref.at[1], out_hbm.at[1]),
        (out_ref.at[2], out_hbm.at[2]),
        (out_ref.at[3], out_hbm.at[3]),
    )
    copies = [pltpu.make_async_copy(s, d, sems.at[i]) for i, (s, d) in enumerate(pairs)]
    for copy in copies[:7]:
        copy.start()
    begin = begin_ref[0]
    for copy in copies[:3]:
        copy.wait()
    _, last_start = start_row(doc_ref, begin)
    dt, total = head_rows(dt_ref, rate_ref)
    final = total[:, ROWS - 1 :]
    pos = begin + lax.broadcasted_iota(jnp.int32, (GROUP_HEADS, ROWS), 1)
    tail = jnp.where(pos >= last_start, jnp.exp(final - total) * dt, 0.0)
    tail = spread_heads(tail)
    whole = jnp.broadcast_to(final, (GROUP_HEADS, ROWS))
    transmit = jnp.where(last_start < begin, jnp.exp(whole), 0.0)
    parts = three_parts(spread_heads(transmit)[:16])
    row = lax.broadcasted_iota(jnp.int32, (16, GROUP_HEADS * HALF), 0)
    sent = jnp.where(
        row == 0,
        parts[0].astype(F32),
        jnp.where(row == 1, parts[1].astype(F32), parts[2].astype(F32)),
    ).astype(BF16)
    copies[3].wait()
    turned = jnp.transpose(b_ref[...])
    copies[4].wait()
    width = GROUP_HEADS * HALF // PEERS
    for j in range(PEERS):
        at = slice(j * width, (j + 1) * width)
        scaled = (x_ref[:, at].astype(F32) * tail[:, at]).astype(BF16)
        out_ref[j, :STATE, :] = dot(turned, scaled).astype(BF16)
        out_ref[j, STATE:, :] = sent[:, at]
        copies[8 + j].start()
    for copy in copies[5:7]:
        copy.wait()
    copies[7].start()
    for copy in copies[7:]:
        copy.wait()


def received(ref, j):
    state = ref[j, :STATE, :].astype(F32)
    parts = ref[j, STATE:, :].astype(F32)
    return state, parts[0:1] + parts[1:2] + parts[2:3]


def pair_up(kv_ref, near_ref, pair_ref):
    pair_ref[:ROWS, :] = kv_ref[...]
    pair_ref[ROWS:, :] = near_ref[...]


def group_state(got_ref, kv_ref, near_ref, own_ref, out_ref):
    del near_ref, own_ref
    total, _ = received(got_ref, 0)
    for j in range(1, PEERS):
        state, transmit = received(got_ref, j)
        total = total * transmit + state
    out_ref[:STATE, :] = total.astype(BF16)
    out_ref[STATE:, :] = kv_ref[...]


def own_parts(got_ref, group_ref, part_ref, factor_ref):
    del group_ref
    part, factor = received(got_ref, 0)
    for j in range(1, PEERS):
        part_ref[j - 1] = part
        factor_ref[j - 1] = jnp.broadcast_to(factor, factor_ref.shape[1:])
        if j < PEERS - 1:
            state, transmit = received(got_ref, j)
            part, factor = part * transmit + state, factor * transmit


def carried_states(part_ref, factor_ref, before_ref, out_hbm, out_ref, sems):
    copies = [
        pltpu.make_async_copy(out_ref.at[j], out_hbm.at[j], sems.at[j]) for j in range(PEERS)
    ]
    out_ref[0] = before_ref[:STATE, :]
    copies[0].start()
    before = before_ref[:STATE, :].astype(F32)
    for j in range(1, PEERS):
        out_ref[j] = (before * factor_ref[j - 1, :1] + part_ref[j - 1]).astype(BF16)
        copies[j].start()
    for copy in copies:
        copy.wait()


def start_columns(doc_ref, begin):
    found, _ = start_row(doc_ref, begin)
    return jnp.transpose(jnp.broadcast_to(found[:1].astype(F32), (ROWS, ROWS)))


def inside(
    begin_ref,
    doc_ref,
    rate_ref,
    x_ref,
    b_ref,
    c_ref,
    dt_ref,
    gate_ref,
    gain_ref,
    own_ref,
    factor_ref,
    gain_out_ref,
):
    begin = begin_ref[0]
    gain_out_ref[...] = gain_ref[...]
    starts = start_columns(doc_ref, begin)
    row = lax.broadcasted_iota(jnp.int32, (ROWS, ROWS), 0)
    lane = lax.broadcasted_iota(jnp.int32, (ROWS, ROWS), 1)
    allowed = (lane <= row) & ((begin + lane).astype(F32) >= starts)
    continued = starts < begin.astype(F32)
    dt, total = head_rows(dt_ref, rate_ref)
    tall = jnp.transpose(jnp.concatenate([total, jnp.zeros((ROWS - GROUP_HEADS, ROWS), F32)], 0))
    inner = dot(c_ref[...], b_ref[...], ((1,), (1,)))
    left = lane < HALF
    for pair in range(GROUP_HEADS // 2):
        at = slice(pair * ROWS, (pair + 1) * ROWS)
        columns, mixing = [], []
        for h in (2 * pair, 2 * pair + 1):
            column = jnp.broadcast_to(tall[:, h : h + 1], (ROWS, ROWS))
            spread = jnp.where(allowed, column - total[h : h + 1], NEG)
            mixing.append((jnp.exp(spread) * dt[h : h + 1] * inner).astype(BF16))
            columns.append(column)
        x = x_ref[:, at]
        zero = jnp.zeros_like(x)
        blocks = jnp.concatenate([jnp.where(left, x, zero), jnp.where(left, zero, x)], 0)
        own = dot(jnp.concatenate(mixing, 1), blocks)
        entry = jnp.where(continued, jnp.exp(jnp.where(left, columns[0], columns[1])), 0.0)
        gate = gate_ref[:, at].astype(F32)
        gate = gate / (1.0 + jnp.exp(-gate))
        own_ref[:, at] = own * gate
        factor_ref[:, at] = entry * gate


def attention(begin_ref, doc_ref, q_ref, kv0_ref, kv2_ref, pair_ref, kv4_ref, out_ref):
    begin = begin_ref[0]
    starts = start_columns(doc_ref, begin)
    row = lax.broadcasted_iota(jnp.int32, (ROWS, ROWS), 0)
    lane = lax.broadcasted_iota(jnp.int32, (ROWS, ROWS), 1)
    blocks = [kv0_ref[...], pair_ref[:ROWS, :], kv2_ref[...], pair_ref[ROWS:, :], kv4_ref[STATE:, :]]
    bias = []
    for j in range(len(blocks)):
        allowed = (begin - j * ROWS + lane).astype(F32) >= starts
        if j == 0:
            allowed = allowed & (lane <= row)
        bias.append(jnp.where(allowed, 0.0, NEG))
    bias = jnp.concatenate(bias, 1)
    keys = jnp.concatenate([b[:, :ROWS] for b in blocks], 0)
    values = jnp.concatenate([b[:, ROWS:] for b in blocks], 0)
    for h in range(Q_HEADS):
        at = slice(h * ROWS, (h + 1) * ROWS)
        scores = dot(q_ref[:, at], keys, ((1,), (1,))) * SCALE + bias
        top = jnp.max(scores, axis=1, keepdims=True)
        probs = jnp.exp(scores - top)
        total = jnp.sum(probs, axis=1, keepdims=True)
        out_ref[:, at] = (dot(probs.astype(BF16), values) / total).astype(BF16)


def finish(c_ref, carried_ref, own_ref, factor_ref, weight_ref, att_ref, out_ref, scratch_ref):
    width = GROUP_HEADS * HALF // PEERS
    squares = jnp.zeros((ROWS, 1), F32)
    c = c_ref[...]
    for j in range(PEERS):
        at = slice(j * width, (j + 1) * width)
        gated = own_ref[:, at] + factor_ref[:, at] * dot(c, carried_ref[j])
        scratch_ref[:, at] = gated
        squares = squares + jnp.sum(gated * gated, axis=1, keepdims=True)
    scale = lax.rsqrt(squares * (1.0 / (GROUP_HEADS * HALF)) + 1e-05)
    for j in range(PEERS):
        at = slice(j * width, (j + 1) * width)
        out_ref[:, at] = (scratch_ref[:, at] * scale * weight_ref[:, at]).astype(BF16)
    out_ref[:, GROUP_HEADS * HALF :] = att_ref[...]


def lay_out(got_ref, mixed_ref, attended_ref):
    width = GROUP_HEADS * HALF
    for j in range(got_ref.shape[0]):
        mixed_ref[:, j * width : (j + 1) * width] = got_ref[j, :, :width]
        attended_ref[:, j * width : (j + 1) * width] = got_ref[j, :, width:]


def local(doc, x, gate, b, c, dt, rate, weight, q, k, v):
    width = GROUP_HEADS * HALF
    tp = lax.axis_size("tp")
    block = lax.axis_index("z") * PEERS + lax.axis_index("x")
    begin = jnp.reshape(block * ROWS, (1,)).astype(jnp.int32)
    dt = dt.T
    own_states, kv = call(
        prepare,
        (shaped((PEERS, STATE + 16, width // PEERS), BF16), shaped((ROWS, 2 * ROWS), BF16)),
        [SMEM] + [HBM] * 7,
        flops=10**8,
        moved=10**6,
        scratch=(
            pltpu.SMEM(doc.shape, jnp.int32),
            pltpu.SMEM(rate.shape, F32),
            pltpu.VMEM(dt.shape, F32),
            pltpu.VMEM(x.shape, BF16),
            pltpu.VMEM(b.shape, BF16),
            pltpu.VMEM((ROWS, 2 * ROWS), BF16),
            pltpu.VMEM((PEERS, STATE + 16, width // PEERS), BF16),
            pltpu.SemaphoreType.DMA((12,)),
        ),
        grant=None,
        out=HBM,
    )(begin, doc, rate, dt, x, b, k, v)
    got = lax.all_to_all(own_states, "x", 0, 0, tiled=True)

    def along(a, distance):
        count = lax.axis_size("z") * PEERS
        return lax.ppermute(a, ("z", "x"), [(i - distance, i) for i in range(distance, count)])

    kv2 = along(kv, 2)
    pair = call(pair_up, shaped((2 * ROWS, 2 * ROWS), BF16), [VMEM] * 2, moved=10**8)(kv, kv2)
    pair = along(pair, 1)
    own, factor, gain = call(
        inside,
        (shaped((ROWS, width), F32), shaped((ROWS, width), F32), shaped((1, width), F32)),
        [SMEM, SMEM, SMEM] + [VMEM] * 6,
        flops=10**8,
        moved=10**6,
        exps=400000,
    )(begin, doc, rate, x, b, c, dt, gate, weight.reshape(1, width))
    group = call(
        group_state,
        shaped((STATE + ROWS, width // PEERS), BF16),
        [VMEM] * 2 + [LATER] * 2,
        flops=10**6,
        moved=10**6,
    )(got, kv, kv2, own)
    before = lax.ppermute(group, "z", [(i - 1, i) for i in range(1, lax.axis_size("z"))])
    part, factors = call(
        own_parts,
        (
            shaped((PEERS - 1, STATE, width // PEERS), F32),
            shaped((PEERS - 1, 8, width // PEERS), F32),
        ),
        [VMEM, LATER],
        flops=10**6,
        moved=10**6,
    )(got, group)
    carried = call(
        carried_states,
        shaped((PEERS, STATE, width // PEERS), BF16),
        [VMEM] * 3,
        flops=10**6,
        moved=10**6,
        scratch=(
            pltpu.VMEM((PEERS, STATE, width // PEERS), BF16),
            pltpu.SemaphoreType.DMA((PEERS,)),
        ),
        out=HBM,
    )(part, factors, before)
    carried = lax.all_to_all(carried, "x", 0, 0, tiled=True)
    att = call(
        attention,
        shaped((ROWS, width), BF16),
        [SMEM, SMEM] + [VMEM] * 5,
        flops=10**10,
        moved=10**8,
        exps=10**8,
    )(begin, doc, q, kv, kv2, pair, before)
    rows = pl.pallas_call(
        finish,
        out_shape=shaped((ROWS, 2 * width), BF16),
        in_specs=[VMEM] * 6,
        out_specs=VMEM,
        scratch_shapes=[pltpu.VMEM((ROWS, width), F32)],
        compiler_params=pltpu.CompilerParams(vmem_limit_bytes=32 * 2**20),
        cost_estimate=pl.CostEstimate(flops=10**8, bytes_accessed=10**6, transcendentals=128),
    )(c, carried, own, factor, gain, att)
    moved = lax.all_to_all(rows.reshape(tp, ROWS // tp, 2 * width), "tp", 0, 0, tiled=True)
    return call(
        lay_out,
        (shaped((ROWS // tp, tp * width), BF16), shaped((ROWS // tp, tp * width), BF16)),
        [VMEM],
        moved=10**6,
    )(moved)


def solution(mesh):
    sizes = dict(mesh.shape)
    inner = Mesh(
        mesh.devices.reshape(sizes["ctx"] // PEERS, PEERS, sizes["tp"]), ("z", "x", "tp")
    )
    both = P(("z", "x"), "tp")
    return jax.shard_map(
        local,
        mesh=inner,
        in_specs=(P(), both, both, both, both, both, P("tp"), P("tp"), both, both, both),
        out_specs=(P(("z", "x", "tp"), None), P(("z", "x", "tp"), None)),
        check_vma=False,
    )
```
